128 devices in a mesh: row: 8 (over z, y_hi), col: 16 (over x, y_lo, core).
Axes of the slice: x: 4, y: 4 (y_hi: 2, y_lo: 2; y = y_hi * 2 + y_lo), z: 4, core: 2. Of those that a mesh axis runs over, the one named last changes fastest.
Arguments:
- left: bfloat16 [16, 32, 2048], P('col', None, 'row'), may hold values from -6 to 6
- right: bfloat16 [16, 32, 2048], P('row', None, 'col'), may hold values from -6 to 6
- pair_grad: bfloat16 [2048, 2048, 128], P('row', 'col'), may hold values from -3 to 3
- w_out: bfloat16 [1024, 128], replicated, may hold values from -0.1875 to 0.1875
Outputs:
- d_left: float32 [16, 32, 2048], P('col', None, 'row')
- d_right: float32 [16, 32, 2048], P('row', None, 'col')
- d_wout: float32 [1024, 128], replicated
The draws below stay inside these ranges and needn't reach their ends.
All inputs are finite; a program needn't handle non-finite values.
Results may differ from the reference program's by a relative error of at most 0.0095.
Values may be sent and summed in bfloat16 or wider, within the bound.
A program may use at most 192 MiB of HBM per device.

```python
import jax
import jax.numpy as jnp
from jax import lax

S = 16
C = 32
H = 128
I = 2048
J = 2048


def steps_of(stream_key, extent, shards, low, high):
    loudness = 1.0
    for axis_at, blocks in shards:
        heights = jax.random.uniform(jax.random.fold_in(jax.random.fold_in(stream_key, 6), axis_at), (blocks,), jnp.float32, low / len(shards), high / len(shards))
        loudness = loudness * jnp.repeat(jnp.exp(heights), extent[axis_at] // blocks).reshape((-1,) + (1,) * (len(extent) - 1 - axis_at))
    return loudness


def bell_draw(key, extent, deviation, most, cuts=(), kind=jnp.bfloat16):
    array = jax.random.normal(key, extent, jnp.float32) * deviation
    if len(cuts) > 0:
        array = steps_of(key, extent, cuts, -0.22, 0.18) * array
    return jnp.clip(array, min=-most, max=most).astype(kind)


def setup_inputs(seed: int = 0) -> dict:
    splits = jax.random.split(jax.random.key(seed), 5)
    return {
        "left": bell_draw(splits[0], (S, C, I), 1.0, 6.0, ((0, 16), (2, 8))),
        "right": bell_draw(splits[1], (S, C, J), 1.0, 6.0, ((0, 8), (2, 16))),
        "pair_grad": bell_draw(splits[2], (I, J, H), 0.5, 3.0, ((0, 8), (1, 16))),
        "w_out": bell_draw(splits[3], (C * C, H), (C * C) ** -0.5, 0.1875),
    }


def reference(left, right, pair_grad, w_out):
    cube = w_out.reshape(C, C, H).astype(jnp.float32)
    left32 = left.astype(jnp.float32)
    right32 = right.astype(jnp.float32)
    ublock = jnp.einsum('sej,ceh->jhsc', right32, cube).astype(jnp.bfloat16).reshape(J * H, S * C)
    block = min(I, 256)
    count = I // block

    def one_block(carry, index):
        acc_right, acc_weight = carry
        begin = (index * block).astype(jnp.int32)
        tile = lax.dynamic_slice_in_dim(pair_grad, begin, block, 0)
        left_part = lax.dynamic_slice_in_dim(left32, begin, block, 2)
        part_left = jnp.dot(tile.reshape(block, J * H), ublock, preferred_element_type=jnp.float32)
        wblock = jnp.einsum('sci,ceh->ihse', left_part, cube).astype(jnp.bfloat16)
        acc_right = acc_right + jnp.einsum('ijh,ihse->jse', tile.astype(jnp.float32), wblock.astype(jnp.float32))
        vblock = jnp.einsum('ijh,sej->ihse', tile.astype(jnp.float32), right32).astype(jnp.bfloat16)
        acc_weight = acc_weight + jnp.einsum('sci,ihse->ceh', left_part, vblock.astype(jnp.float32))
        return (acc_right, acc_weight), part_left

    start = (jnp.zeros((J, S, C), jnp.float32), jnp.zeros((C, C, H), jnp.float32))
    (acc_right, acc_weight), parts = lax.scan(one_block, start, jnp.arange(count, dtype=jnp.int32))
    grad_left = parts.reshape(I, S, C).transpose(1, 2, 0) * (1.0 / S)
    grad_right = acc_right.transpose(1, 2, 0) * (1.0 / S)
    grad_weight = acc_weight.reshape(C * C, H) * (1.0 / (float(I) * float(J)) ** 0.5)
    return grad_left, grad_right, grad_weight
```

```python
import functools

import jax
import jax.numpy as jnp
from jax import lax
from jax.experimental import pallas as pl
from jax.experimental.pallas import tpu as pltpu
from jax.sharding import PartitionSpec as P

BF, F32 = jnp.bfloat16, jnp.float32
MESH = pl.DeviceIdType.MESH
S, C, H = 16, 32, 128
IL, JL = 256, 128
NR, NC = 8, 16
JB = 16
NB = JL // JB
BLK = JB * S


def dot_nn(a, b):
    return jnp.dot(a, b, preferred_element_type=F32)


def dot_nt(a, b):
    return lax.dot_general(a, b, (((1,), (1,)), ((), ())), preferred_element_type=F32)


def loop(lower, upper, body):
    def step(k, carry):
        body(k)
        return carry

    lax.fori_loop(lower, upper, step, 0)


def kernel(
    scale_weight,
    left_hbm, right_hbm, g_hbm, w_hbm,
    dl_out, dr_out, dw_out,
    w_v, lg, rg, g_in, gt, lf, lb, rf, rb, rt, w1, wt, tb, ub,
    drf, drs, drr, dwa, dws, dwr1, dwp, dws2, dwr2, dwp2, dwg, dla, dls, dlr,
    g_sem, in_sem,
    agl_s, agl_r, agr_s, agr_r, rsr_s, rsr_r, w1_s, w1_r, w2_s, w2_r, w3_s, w3_r, w4_s, w4_r, rsl_s, rsl_r,
):
    me_r = lax.axis_index("row")
    me_c = lax.axis_index("col")

    def row_peer(d):
        return lax.rem(me_r + d, NR)

    def col_peer(d):
        return lax.rem(me_c + d, NC)

    def to_row(src, dst, send, recv, d):
        return pltpu.make_async_remote_copy(
            src_ref=src, dst_ref=dst, send_sem=send.at[d - 1], recv_sem=recv.at[d - 1],
            device_id=(row_peer(d), me_c), device_id_type=MESH,
        )

    def to_col(src, dst, send, recv, d):
        return pltpu.make_async_remote_copy(
            src_ref=src, dst_ref=dst, send_sem=send.at[d - 1], recv_sem=recv.at[d - 1],
            device_id=(me_r, col_peer(d)), device_id_type=MESH,
        )

    barrier = pltpu.get_barrier_semaphore()
    loop(1, NR, lambda d: pl.semaphore_signal(barrier, inc=1, device_id=(row_peer(d), me_c), device_id_type=MESH))
    loop(1, NC, lambda d: pl.semaphore_signal(barrier, inc=1, device_id=(me_r, col_peer(d)), device_id_type=MESH))

    def g_copy(b):
        at = pl.multiple_of(b * JB, JB)
        return pltpu.make_async_copy(g_hbm.at[:, pl.ds(at, JB), :], g_in.at[b], g_sem.at[b])

    local = [
        pltpu.make_async_copy(w_hbm, w_v, in_sem.at[0]),
        pltpu.make_async_copy(left_hbm.at[0], lg.at[me_c], in_sem.at[1]),
        pltpu.make_async_copy(right_hbm, rg.at[pl.ds(2 * me_r, 2)], in_sem.at[2]),
    ]
    for copy in local:
        copy.start()
    loop(0, NB, lambda b: g_copy(b).start())
    pl.semaphore_wait(barrier, NR - 1 + NC - 1)

    def gather_left(d):
        return to_col(left_hbm.at[0], lg.at[me_c], agl_s, agl_r, d)

    def gather_right(d):
        return to_row(right_hbm, rg.at[pl.ds(2 * me_r, 2)], agr_s, agr_r, d)

    loop(1, NC, lambda d: gather_left(d).start())
    loop(1, NR, lambda d: gather_right(d).start())

    local[0].wait()
    for c in range(C):
        w1[:, c * H : (c + 1) * H] = w_v[c * C : (c + 1) * C, :]
        block = w_v[c * C : (c + 1) * C, :].astype(F32)
        wt[c * H : (c + 1) * H, :] = jnp.concatenate([block, jnp.zeros((128 - C, H), F32)], 0).T.astype(BF)
    dwa[...] = jnp.zeros_like(dwa)
    dla[...] = jnp.zeros_like(dla)

    def turn(b):
        g_copy(b).wait()
        for q in range(IL // 16):
            gt[b, :, q * 16 : (q + 1) * 16, :] = jnp.swapaxes(g_in[b, q * 16 : (q + 1) * 16], 0, 1)

    loop(0, NB, turn)

    local[2].wait()
    loop(1, NR, lambda d: gather_right(d).wait())
    for s in range(S):
        block = jnp.concatenate([rg[s].astype(F32), jnp.zeros((128 - C, JL), F32)], 0)
        rf[pl.ds(s, JL, stride=S), :] = block.T
    rb[...] = rf[...].astype(BF)

    def right_turned(b):
        at = pl.multiple_of(b * BLK, BLK)
        rt[:, pl.ds(at, BLK)] = rf[pl.ds(at, BLK), :].T[:C].astype(BF)

    loop(0, NB, right_turned)

    local[1].wait()
    loop(1, NC, lambda d: gather_left(d).wait())
    for s in range(S):
        for k in range(2):
            lf[k, pl.ds(s, C, stride=S), :] = lg[s, :, k * 128 : (k + 1) * 128].astype(F32)
    for k in range(2):
        lb[:, k * 128 : (k + 1) * 128] = lf[k].astype(BF)

    def phase1(b):
        at = pl.multiple_of(b * BLK, BLK)
        for p in range(JB // 2):
            rhs = jnp.concatenate([gt[b, 2 * p], gt[b, 2 * p + 1]], 1)
            t = dot_nn(lb[...], rhs).astype(BF)
            for k in range(2):
                j = 2 * p + k
                for c in range(C):
                    tb[j * S : (j + 1) * S, c * H : (c + 1) * H] = t[c * S : (c + 1) * S, k * H : (k + 1) * H]
        dwa[...] += dot_nn(rt[:, pl.ds(at, BLK)], tb[...])
        drf[pl.ds(at, BLK), :] = dot_nn(tb[...], wt[...])

    loop(0, NB, phase1)

    for c in range(C):
        dws[c * C : (c + 1) * C, :] = dwa[:, c * H : (c + 1) * H].astype(BF)

    def weight_rows(k):
        return pl.ds(pl.multiple_of(k * 64, 64), 64)

    def weight1(d):
        return to_col(dws.at[weight_rows(col_peer(d))], dwr1.at[d - 1], w1_s, w1_r, d)

    loop(1, NC, lambda d: weight1(d).start())
    for s in range(S):
        drs[s] = drf[pl.ds(s, JL, stride=S), :].T[:C].astype(BF)

    def reduce_right(d):
        return to_row(drs.at[pl.ds(2 * row_peer(d), 2)], drr.at[d - 1], rsr_s, rsr_r, d)

    loop(1, NR, lambda d: reduce_right(d).start())

    def weight2(d):
        return to_row(dws2.at[row_peer(d)], dwr2.at[d - 1], w2_s, w2_r, d)

    def weight3(d):
        return to_row(dwp2, dwp.at[me_r], w3_s, w3_r, d)

    def weight4(d):
        return to_col(dwg.at[weight_rows(me_c)], dwg.at[weight_rows(me_c)], w4_s, w4_r, d)

    def stage_a():
        loop(1, NC, lambda d: weight1(d).wait())
        total = dws[weight_rows(me_c), :].astype(F32)
        for k in range(NC - 1):
            total += dwr1[k].astype(F32)
        dws2[...] = total.reshape(NR, 8, H)
        loop(1, NR, lambda d: weight2(d).start())

    def stage_b():
        loop(1, NR, lambda d: weight2(d).wait())
        total = dws2[me_r]
        for k in range(NR - 1):
            total += dwr2[k]
        total = total * scale_weight
        dwp2[...] = total
        dwp[me_r] = total
        loop(1, NR, lambda d: weight3(d).start())

    def stage_c():
        loop(1, NR, lambda d: weight3(d).wait())
        dwg[weight_rows(me_c), :] = dwp[...].reshape(64, H).astype(BF)
        loop(1, NC, lambda d: weight4(d).start())

    def stage_d():
        loop(1, NR, lambda d: reduce_right(d).wait())
        total = drs[pl.ds(2 * me_r, 2)].astype(F32)
        for k in range(NR - 1):
            total += drr[k].astype(F32)
        dr_out[...] = total * (1.0 / S)

    def phase2(b):
        at = pl.multiple_of(b * BLK, BLK)
        for q in range(4):
            u = dot_nn(rb[pl.ds(at, BLK), :C], w1[:, q * 1024 : (q + 1) * 1024]).astype(BF)
            for j in range(JB):
                for c in range(8):
                    row = (q * 8 + c) * S
                    ub[row : row + S, j * H : (j + 1) * H] = u[j * S : (j + 1) * S, c * H : (c + 1) * H]
        rhs = jnp.concatenate([gt[b, j] for j in range(JB)], 1)
        part = dot_nt(ub[...], rhs)
        for k in range(2):
            dla[k] += part[:, k * 128 : (k + 1) * 128]
        pl.when(b == 2)(stage_a)
        pl.when(b == 4)(stage_b)
        pl.when(b == 5)(stage_c)
        pl.when(b == 6)(stage_d)

    loop(0, NB, phase2)

    for s in range(S):
        for k in range(2):
            dls[s, :, k * 128 : (k + 1) * 128] = dla[k, pl.ds(s, C, stride=S), :].astype(BF)

    def reduce_left(d):
        return to_col(dls.at[col_peer(d)], dlr.at[d - 1], rsl_s, rsl_r, d)

    loop(1, NC, lambda d: reduce_left(d).start())
    loop(1, NC, lambda d: weight4(d).wait())
    dw_out[...] = dwg[...].astype(F32)
    loop(1, NC, lambda d: reduce_left(d).wait())
    total = dls[me_c].astype(F32)
    for k in range(NC - 1):
        total += dlr[k].astype(F32)
    dl_out[0] = total * (1.0 / S)


def on_device(left, right, pair_grad, w_out):
    total_rows = pair_grad.shape[0] * lax.axis_size("row")
    total_cols = pair_grad.shape[1] * lax.axis_size("col")
    scale_weight = 1.0 / (float(total_rows) * float(total_cols)) ** 0.5
    sems = [pltpu.SemaphoreType.DMA((n - 1,)) for n in (NC, NR, NR, NC, NR, NR, NC, NC) for _ in range(2)]
    return pl.pallas_call(
        functools.partial(kernel, scale_weight),
        out_shape=(
            jax.ShapeDtypeStruct((1, C, IL), F32),
            jax.ShapeDtypeStruct((2, C, JL), F32),
            jax.ShapeDtypeStruct((C * C, H), F32),
        ),
        in_specs=[pl.BlockSpec(memory_space=pl.ANY)] * 4,
        out_specs=[pl.BlockSpec(memory_space=pltpu.VMEM)] * 3,
        scratch_shapes=[
            pltpu.VMEM((C * C, H), BF),
            pltpu.VMEM((S, C, IL), BF),
            pltpu.VMEM((S, C, JL), BF),
            pltpu.VMEM((NB, IL, JB, H), BF),
            pltpu.VMEM((NB, JB, IL, H), BF),
            pltpu.VMEM((2, C * S, 128), F32),
            pltpu.VMEM((C * S, IL), BF),
            pltpu.VMEM((JL * S, 128), F32),
            pltpu.VMEM((JL * S, 128), BF),
            pltpu.VMEM((C, JL * S), BF),
            pltpu.VMEM((C, C * H), BF),
            pltpu.VMEM((C * H, 128), BF),
            pltpu.VMEM((BLK, C * H), BF),
            pltpu.VMEM((C * S, JB * H), BF),
            pltpu.VMEM((JL * S, 128), F32),
            pltpu.VMEM((S, C, JL), BF),
            pltpu.VMEM((NR - 1, 2, C, JL), BF),
            pltpu.VMEM((C, C * H), F32),
            pltpu.VMEM((C * C, H), BF),
            pltpu.VMEM((NC - 1, 64, H), BF),
            pltpu.VMEM((NR, 8, H), F32),
            pltpu.VMEM((NR, 8, H), F32),
            pltpu.VMEM((NR - 1, 8, H), F32),
            pltpu.VMEM((8, H), F32),
            pltpu.VMEM((C * C, H), BF),
            pltpu.VMEM((2, C * S, 128), F32),
            pltpu.VMEM((S, C, IL), BF),
            pltpu.VMEM((NC - 1, C, IL), BF),
            pltpu.SemaphoreType.DMA((NB,)),
            pltpu.SemaphoreType.DMA((3,)),
            *sems,
        ],
        compiler_params=pltpu.CompilerParams(
            collective_id=0, has_side_effects=True, vmem_limit_bytes=60 * 2**20
        ),
        name="outer_product_mean_grad",
    )(left, right, pair_grad, w_out)


def solution(mesh):
    return jax.shard_map(
        on_device,
        mesh=mesh,
        in_specs=(P("col", None, "row"), P("row", None, "col"), P("row", "col", None), P()),
        out_specs=(P("col", None, "row"), P("row", None, "col"), P()),
        check_vma=False,
    )
```

```python
import functools

import jax
import jax.numpy as jnp
from jax import lax
from jax.experimental import pallas as pl
from jax.experimental.pallas import tpu as pltpu
from jax.sharding import PartitionSpec as P

BF, F32 = jnp.bfloat16, jnp.float32
MESH = pl.DeviceIdType.MESH
S, C, H = 16, 32, 128
IL, JL = 256, 128
NR, NC = 8, 16
JB = 16
NB = JL // JB
BLK = JB * S
NU = 3
STAGE_A, STAGE_B = 5, 3


def dot_nn(a, b):
    return jnp.dot(a, b, preferred_element_type=F32)


def dot_nt(a, b):
    return lax.dot_general(a, b, (((1,), (1,)), ((), ())), preferred_element_type=F32)


def loop(lower, upper, body):
    def step(k, carry):
        body(k)
        return carry

    lax.fori_loop(lower, upper, step, 0)


def kernel(
    scale_weight,
    left_hbm, right_hbm, g_hbm, w_hbm,
    dl_out, dr_out, dw_out,
    w_v, lg, rg, g_in, gt, lf, lb, rf, rb, rt, w1, wt, tb, ub,
    drf, drs, drr, dwa, dws, dwr1, dwr2, dwg, dla, dls, dlr,
    g_sem, in_sem,
    agl_s, agl_r, agr_s, agr_r, rsr_s, rsr_r, w1_s, w1_r, w2_s, w2_r, w3_s, w3_r, rsl_s, rsl_r,
):
    me_r = lax.axis_index("row")
    me_c = lax.axis_index("col")

    def row_peer(d):
        return lax.rem(me_r + d, NR)

    def col_peer(d):
        return lax.rem(me_c + d, NC)

    def to_row(src, dst, send, recv, d):
        return pltpu.make_async_remote_copy(
            src_ref=src, dst_ref=dst, send_sem=send.at[d - 1], recv_sem=recv.at[d - 1],
            device_id=(row_peer(d), me_c), device_id_type=MESH,
        )

    def to_col(src, dst, send, recv, d):
        return pltpu.make_async_remote_copy(
            src_ref=src, dst_ref=dst, send_sem=send.at[d - 1], recv_sem=recv.at[d - 1],
            device_id=(me_r, col_peer(d)), device_id_type=MESH,
        )

    barrier = pltpu.get_barrier_semaphore()
    loop(1, NR, lambda d: pl.semaphore_signal(barrier, inc=1, device_id=(row_peer(d), me_c), device_id_type=MESH))
    loop(1, NC, lambda d: pl.semaphore_signal(barrier, inc=1, device_id=(me_r, col_peer(d)), device_id_type=MESH))

    def g_copy(b):
        at = pl.multiple_of(b * JB, JB)
        return pltpu.make_async_copy(g_hbm.at[:, pl.ds(at, JB), :], g_in.at[b], g_sem.at[b])

    local = [
        pltpu.make_async_copy(w_hbm, w_v, in_sem.at[0]),
        pltpu.make_async_copy(left_hbm.at[0], lg.at[me_c], in_sem.at[1]),
        pltpu.make_async_copy(right_hbm, rg.at[pl.ds(2 * me_r, 2)], in_sem.at[2]),
    ]
    for copy in local:
        copy.start()
    loop(0, NB, lambda b: g_copy(b).start())
    pl.semaphore_wait(barrier, NR - 1 + NC - 1)

    def gather_left(d):
        return to_col(left_hbm.at[0], lg.at[me_c], agl_s, agl_r, d)

    def gather_right(d):
        return to_row(right_hbm, rg.at[pl.ds(2 * me_r, 2)], agr_s, agr_r, d)

    loop(1, NR, lambda d: gather_right(d).start())
    loop(1, NC, lambda d: gather_left(d).start())

    local[0].wait()
    for c in range(C):
        w1[:, c * H : (c + 1) * H] = w_v[c * C : (c + 1) * C, :]
        block = w_v[c * C : (c + 1) * C, :].astype(F32)
        wt[c * H : (c + 1) * H, :] = jnp.concatenate([block, jnp.zeros((128 - C, H), F32)], 0).T.astype(BF)
    dwa[...] = jnp.zeros_like(dwa)
    dla[...] = jnp.zeros_like(dla)

    def turn(b):
        g_copy(b).wait()
        for q in range(IL // 16):
            gt[b, :, q * 16 : (q + 1) * 16, :] = jnp.swapaxes(g_in[b, q * 16 : (q + 1) * 16], 0, 1)

    loop(0, NB, turn)

    local[2].wait()
    loop(1, NR, lambda d: gather_right(d).wait())
    for s in range(S):
        block = jnp.concatenate([rg[s].astype(F32), jnp.zeros((128 - C, JL), F32)], 0)
        rf[pl.ds(s, JL, stride=S), :] = block.T
    rb[...] = rf[...].astype(BF)

    def right_turned(b):
        at = pl.multiple_of(b * BLK, BLK)
        rt[:, pl.ds(at, BLK)] = rf[pl.ds(at, BLK), :].T[:C].astype(BF)

    loop(0, NB, right_turned)

    def make_u(b):
        at = pl.multiple_of(b * BLK, BLK)
        slot = lax.rem(b, NU)
        for q in range(4):
            u = dot_nn(rb[pl.ds(at, BLK), :C], w1[:, q * 1024 : (q + 1) * 1024]).astype(BF)
            for j in range(JB):
                for c in range(8):
                    row = (q * 8 + c) * S
                    ub[slot, row : row + S, j * H : (j + 1) * H] = u[j * S : (j + 1) * S, c * H : (c + 1) * H]

    loop(0, NU, make_u)

    local[1].wait()
    loop(1, NC, lambda d: gather_left(d).wait())
    for s in range(S):
        for k in range(2):
            lf[k, pl.ds(s, C, stride=S), :] = lg[s, :, k * 128 : (k + 1) * 128].astype(F32)
    for k in range(2):
        lb[:, k * 128 : (k + 1) * 128] = lf[k].astype(BF)

    def phase1(b):
        at = pl.multiple_of(b * BLK, BLK)
        for p in range(JB // 2):
            rhs = jnp.concatenate([gt[b, 2 * p], gt[b, 2 * p + 1]], 1)
            t = dot_nn(lb[...], rhs).astype(BF)
            for k in range(2):
                j = 2 * p + k
                for c in range(C):
                    tb[b, j * S : (j + 1) * S, c * H : (c + 1) * H] = t[c * S : (c + 1) * S, k * H : (k + 1) * H]
        dwa[...] += dot_nn(rt[:, pl.ds(at, BLK)], tb[b])

    loop(0, NB, phase1)

    for c in range(C):
        dws[c * C : (c + 1) * C, :] = dwa[:, c * H : (c + 1) * H].astype(BF)

    def weight_rows(k):
        return pl.ds(pl.multiple_of(k * 64, 64), 64)

    def weight1(d):
        return to_col(dws.at[weight_rows(col_peer(d))], dwr1.at[d - 1], w1_s, w1_r, d)

    def weight2(d):
        return to_row(dwr2.at[me_r], dwr2.at[me_r], w2_s, w2_r, d)

    def weight3(d):
        return to_col(dwg.at[weight_rows(me_c)], dwg.at[weight_rows(me_c)], w3_s, w3_r, d)

    loop(1, NC, lambda d: weight1(d).start())

    def stage_a():
        loop(1, NC, lambda d: weight1(d).wait())
        total = dws[weight_rows(me_c), :].astype(F32)
        for k in range(NC - 1):
            total += dwr1[k].astype(F32)
        dwr2[me_r] = (total * scale_weight).astype(BF)
        loop(1, NR, lambda d: weight2(d).start())

    def stage_b():
        loop(1, NR, lambda d: weight2(d).wait())
        total = dwr2[0].astype(F32)
        for k in range(1, NR):
            total += dwr2[k].astype(F32)
        dwg[weight_rows(me_c), :] = total.astype(BF)
        loop(1, NC, lambda d: weight3(d).start())

    def phase2(b):
        pl.when(b >= NU)(lambda: make_u(b))
        rhs = jnp.concatenate([gt[b, j] for j in range(JB)], 1)
        part = dot_nt(ub[lax.rem(b, NU)], rhs)
        for k in range(2):
            dla[k] += part[:, k * 128 : (k + 1) * 128]
        pl.when(b == STAGE_A)(stage_a)

    loop(0, NB, phase2)

    for s in range(S):
        for k in range(2):
            dls[s, :, k * 128 : (k + 1) * 128] = dla[k, pl.ds(s, C, stride=S), :].astype(BF)

    def reduce_left(d):
        return to_col(dls.at[col_peer(d)], dlr.at[d - 1], rsl_s, rsl_r, d)

    loop(1, NC, lambda d: reduce_left(d).start())

    def phase3(b):
        at = pl.multiple_of(b * BLK, BLK)
        drf[pl.ds(at, BLK), :] = dot_nn(tb[b], wt[...])
        pl.when(b == STAGE_B)(stage_b)

    loop(0, NB, phase3)

    for s in range(S):
        drs[s] = drf[pl.ds(s, JL, stride=S), :].T[:C].astype(BF)

    def reduce_right(d):
        return to_row(drs.at[pl.ds(2 * row_peer(d), 2)], drr.at[d - 1], rsr_s, rsr_r, d)

    loop(1, NR, lambda d: reduce_right(d).start())

    loop(1, NC, lambda d: reduce_left(d).wait())
    total = dls[me_c].astype(F32)
    for k in range(NC - 1):
        total += dlr[k].astype(F32)
    dl_out[0] = total * (1.0 / S)
    loop(1, NC, lambda d: weight3(d).wait())
    dw_out[...] = dwg[...]
    loop(1, NR, lambda d: reduce_right(d).wait())
    total = drs[pl.ds(2 * me_r, 2)].astype(F32)
    for k in range(NR - 1):
        total += drr[k].astype(F32)
    dr_out[...] = total * (1.0 / S)


def hand_out(a, b, c, x, y, z):
    x[...] = a[...]
    y[...] = b[...]
    z[...] = c[...].astype(F32)


def on_device(left, right, pair_grad, w_out):
    total_rows = pair_grad.shape[0] * lax.axis_size("row")
    total_cols = pair_grad.shape[1] * lax.axis_size("col")
    scale_weight = 1.0 / (float(total_rows) * float(total_cols)) ** 0.5
    sems = [pltpu.SemaphoreType.DMA((n - 1,)) for n in (NC, NR, NR, NC, NR, NC, NC) for _ in range(2)]
    grads = pl.pallas_call(
        functools.partial(kernel, scale_weight),
        out_shape=(
            jax.ShapeDtypeStruct((1, C, IL), F32),
            jax.ShapeDtypeStruct((2, C, JL), F32),
            jax.ShapeDtypeStruct((C * C, H), BF),
        ),
        in_specs=[pl.BlockSpec(memory_space=pl.ANY)] * 4,
        out_specs=[pl.BlockSpec(memory_space=pltpu.VMEM)] * 3,
        scratch_shapes=[
            pltpu.VMEM((C * C, H), BF),
            pltpu.VMEM((S, C, IL), BF),
            pltpu.VMEM((S, C, JL), BF),
            pltpu.VMEM((NB, IL, JB, H), BF),
            pltpu.VMEM((NB, JB, IL, H), BF),
            pltpu.VMEM((2, C * S, 128), F32),
            pltpu.VMEM((C * S, IL), BF),
            pltpu.VMEM((JL * S, 128), F32),
            pltpu.VMEM((JL * S, 128), BF),
            pltpu.VMEM((C, JL * S), BF),
            pltpu.VMEM((C, C * H), BF),
            pltpu.VMEM((C * H, 128), BF),
            pltpu.VMEM((NB, BLK, C * H), BF),
            pltpu.VMEM((NU, C * S, JB * H), BF),
            pltpu.VMEM((JL * S, 128), F32),
            pltpu.VMEM((S, C, JL), BF),
            pltpu.VMEM((NR - 1, 2, C, JL), BF),
            pltpu.VMEM((C, C * H), F32),
            pltpu.VMEM((C * C, H), BF),
            pltpu.VMEM((NC - 1, 64, H), BF),
            pltpu.VMEM((NR, 64, H), BF),
            pltpu.VMEM((C * C, H), BF),
            pltpu.VMEM((2, C * S, 128), F32),
            pltpu.VMEM((S, C, IL), BF),
            pltpu.VMEM((NC - 1, C, IL), BF),
            pltpu.SemaphoreType.DMA((NB,)),
            pltpu.SemaphoreType.DMA((3,)),
            *sems,
        ],
        compiler_params=pltpu.CompilerParams(
            collective_id=0, has_side_effects=True, vmem_limit_bytes=60 * 2**20
        ),
        name="outer_product_mean_grad",
    )(left, right, pair_grad, w_out)
    return pl.pallas_call(
        hand_out,
        out_shape=tuple(jax.ShapeDtypeStruct(g.shape, F32) for g in grads),
        name="hand_out",
    )(*grads)


def solution(mesh):
    return jax.shard_map(
        on_device,
        mesh=mesh,
        in_specs=(P("col", None, "row"), P("row", None, "col"), P("row", "col", None), P()),
        out_specs=(P("col", None, "row"), P("row", None, "col"), P()),
        check_vma=False,
    )
```

```python
import functools

import jax
import jax.numpy as jnp
from jax import lax
from jax.experimental import pallas as pl
from jax.experimental.pallas import tpu as pltpu
from jax.sharding import PartitionSpec as P

BF, F32 = jnp.bfloat16, jnp.float32
MESH = pl.DeviceIdType.MESH
S, C, H = 16, 32, 128
IL, JL = 256, 128
NR, NC = 8, 16
JB = 16
NB = JL // JB
BLK = JB * S
NU = 5
STAGE_A, STAGE_B = 6, 11


push, acc_lhs, pop = pltpu.matmul_push_rhs, pltpu.matmul_acc_lhs, pltpu.matmul_pop


def acc(rows, count):
    return [pltpu.ACC(m)((rows, 256), F32) for m in range(2) for _ in range(count)]


def loop(lower, upper, body):
    def step(k, carry):
        body(k)
        return carry

    lax.fori_loop(lower, upper, step, 0)


def kernel(
    scale_weight,
    left_hbm, right_hbm, g_hbm, w_hbm,
    dl_out, dr_out, dw_out,
    w_v, lg, rg, g_in, gt, lf, lb, rf, rb, rt, w1, wt, tb, ub,
    drf, drs, drr, dws, dwr1, dwr2, dwg, dla, dls, dlr,
    g_sem, in_sem,
    agl_s, agl_r, agr_s, agr_r, rsr_s, rsr_r, w1_s, w1_r, w2_s, w2_r, w3_s, w3_r, rsl_s, rsl_r,
):
    me_r = lax.axis_index("row")
    me_c = lax.axis_index("col")

    def row_peer(d):
        return lax.rem(me_r + d, NR)

    def col_peer(d):
        return lax.rem(me_c + d, NC)

    def to_row(src, dst, send, recv, d):
        return pltpu.make_async_remote_copy(
            src_ref=src, dst_ref=dst, send_sem=send.at[d - 1], recv_sem=recv.at[d - 1],
            device_id=(row_peer(d), me_c), device_id_type=MESH,
        )

    def to_col(src, dst, send, recv, d):
        return pltpu.make_async_remote_copy(
            src_ref=src, dst_ref=dst, send_sem=send.at[d - 1], recv_sem=recv.at[d - 1],
            device_id=(me_r, col_peer(d)), device_id_type=MESH,
        )

    barrier = pltpu.get_barrier_semaphore()
    loop(1, NR, lambda d: pl.semaphore_signal(barrier, inc=1, device_id=(row_peer(d), me_c), device_id_type=MESH))
    loop(1, NC, lambda d: pl.semaphore_signal(barrier, inc=1, device_id=(me_r, col_peer(d)), device_id_type=MESH))

    def g_copy(b):
        at = pl.multiple_of(b * JB, JB)
        return pltpu.make_async_copy(g_hbm.at[:, pl.ds(at, JB), :], g_in.at[b], g_sem.at[b])

    local = [
        pltpu.make_async_copy(w_hbm, w_v, in_sem.at[0]),
        pltpu.make_async_copy(left_hbm.at[0], lg.at[me_c], in_sem.at[1]),
        pltpu.make_async_copy(right_hbm, rg.at[pl.ds(2 * me_r, 2)], in_sem.at[2]),
    ]
    for copy in local:
        copy.start()
    loop(0, NB, lambda b: g_copy(b).start())
    pl.semaphore_wait(barrier, NR - 1 + NC - 1)

    def gather_left(d):
        return to_col(left_hbm.at[0], lg.at[me_c], agl_s, agl_r, d)

    def gather_right(d):
        return to_row(right_hbm, rg.at[pl.ds(2 * me_r, 2)], agr_s, agr_r, d)

    loop(1, NR, lambda d: gather_right(d).start())
    loop(1, NC, lambda d: gather_left(d).start())

    w1[...] = jnp.zeros_like(w1)
    wt[...] = jnp.zeros_like(wt)
    rb[:, 128:] = jnp.zeros_like(rb[:, 128:])
    local[0].wait()
    for c in range(C):
        w1[:C, c * H : (c + 1) * H] = w_v[c * C : (c + 1) * C, :]
        block = w_v[c * C : (c + 1) * C, :].astype(F32)
        wt[c * H : (c + 1) * H, :128] = jnp.concatenate([block, jnp.zeros((128 - C, H), F32)], 0).T.astype(BF)

    def turn(b):
        g_copy(b).wait()
        for q in range(IL // 16):
            gt[b, :, q * 16 : (q + 1) * 16, :] = jnp.swapaxes(g_in[b, q * 16 : (q + 1) * 16], 0, 1)

    loop(0, NB, turn)

    local[2].wait()
    loop(1, NR, lambda d: gather_right(d).wait())
    for s in range(S):
        block = jnp.concatenate([rg[s].astype(F32), jnp.zeros((128 - C, JL), F32)], 0)
        rf[pl.ds(s, JL, stride=S), :] = block.T
    rb[:, :128] = rf[...].astype(BF)

    def right_turned(b):
        at = pl.multiple_of(b * BLK, BLK)
        rt[:, pl.ds(at, BLK)] = rf[pl.ds(at, BLK), :].T[:C].astype(BF)

    loop(0, NB, right_turned)

    def make_u(b, regions):
        at = pl.multiple_of(b * BLK, BLK)
        slot = lax.rem(b, NU)
        pending = []

        def take():
            q = pending.pop(0)
            u = pop(regions[q % 2][q // 2 % 2]).astype(BF)
            for c in range(2):
                for j in range(JB):
                    row = (2 * q + c) * S
                    ub[slot, row : row + S, j * H : (j + 1) * H] = u[j * S : (j + 1) * S, c * H : (c + 1) * H]

        for q in range(C // 2):
            push(w1[:, q * 256 : (q + 1) * 256], q // 2 % 2, q % 2)
            if len(pending) >= 2:
                take()
            acc_lhs(regions[q % 2][q // 2 % 2], rb[pl.ds(at, BLK), :], q // 2 % 2)
            pending.append(q)
        while pending:
            take()

    def early(*accs):
        loop(0, NU, lambda b: make_u(b, (accs[0:2], accs[2:4])))

    pl.run_scoped(early, *acc(256, 2))

    local[1].wait()
    loop(1, NC, lambda d: gather_left(d).wait())
    for s in range(S):
        for k in range(2):
            lf[k, pl.ds(s, C, stride=S), :] = lg[s, :, k * 128 : (k + 1) * 128].astype(F32)
    for k in range(2):
        lb[:, k * 128 : (k + 1) * 128] = lf[k].astype(BF)

    def pair(b, p):
        return jnp.concatenate([gt[b, 2 * p], gt[b, 2 * p + 1]], 1)

    def phase1(*accs):
        t_acc, w_acc = (accs[0:3], accs[3:6]), (accs[6:14], accs[14:22])

        def block(b):
            at = pl.multiple_of(b * BLK, BLK)
            pending, used = [], [0, 0]

            def take():
                region, p, half = pending.pop(0)
                t = pop(region).astype(BF)
                for k in range(2):
                    j = 2 * p + k
                    for c in range(C // 2):
                        cc = half * (C // 2) + c
                        tb[b, j * S : (j + 1) * S, cc * H : (cc + 1) * H] = t[c * S : (c + 1) * S, k * H : (k + 1) * H]

            for p in range(JB // 2):
                m = p % 2
                push(pair(b, p), p // 2 % 2, m)
                for half in range(2):
                    region = t_acc[m][used[m] % 3]
                    used[m] += 1
                    if len(pending) >= 4:
                        take()
                    acc_lhs(region, lb[half * 256 : (half + 1) * 256, :], p // 2 % 2 if half == 0 else None)
                    pending.append((region, p, half))
            while pending:
                take()
            for q in range(C // 2):
                push(tb[b, :, q * 256 : (q + 1) * 256], q // 2 % 2, q % 2)
                acc_lhs(w_acc[q % 2][q // 2], rt[:, pl.ds(at, BLK)], q // 2 % 2)

        loop(0, NB, block)
        for q in range(C // 2):
            part = pop(w_acc[q % 2][q // 2]).astype(BF)
            for k in range(2):
                dws[(2 * q + k) * C : (2 * q + k + 1) * C, :] = part[:, k * H : (k + 1) * H]

    pl.run_scoped(phase1, *acc(256, 3), *acc(C, 8))

    def weight_rows(k):
        return pl.ds(pl.multiple_of(k * 64, 64), 64)

    def weight1(d):
        return to_col(dws.at[weight_rows(col_peer(d))], dwr1.at[d - 1], w1_s, w1_r, d)

    def weight2(d):
        return to_row(dwr2.at[me_r], dwr2.at[me_r], w2_s, w2_r, d)

    def weight3(d):
        return to_col(dwg.at[weight_rows(me_c)], dwg.at[weight_rows(me_c)], w3_s, w3_r, d)

    loop(1, NC, lambda d: weight1(d).start())

    def stage_a():
        loop(1, NC, lambda d: weight1(d).wait())
        total = dws[weight_rows(me_c), :].astype(F32)
        for k in range(NC - 1):
            total += dwr1[k].astype(F32)
        dwr2[me_r] = (total * scale_weight).astype(BF)
        loop(1, NR, lambda d: weight2(d).start())

    def stage_b():
        loop(1, NR, lambda d: weight2(d).wait())
        total = dwr2[0].astype(F32)
        for k in range(1, NR):
            total += dwr2[k].astype(F32)
        dwg[weight_rows(me_c), :] = total.astype(BF)
        loop(1, NC, lambda d: weight3(d).start())

    def phase2(*accs):
        l_acc, u_acc = accs[0:2], (accs[2:4], accs[4:6])

        def block(b):
            pl.when(b >= NU)(lambda: make_u(b, u_acc))
            slot = lax.rem(b, NU)
            for p in range(JB // 2):
                push(pair(b, p), p // 2 % 2, p % 2, transpose=True)
                acc_lhs(l_acc[p % 2], ub[slot, :, p * 256 : (p + 1) * 256], p // 2 % 2)
            pl.when(b == STAGE_A)(stage_a)

        loop(0, NB, block)
        part = pop(l_acc[0]) + pop(l_acc[1])
        for k in range(2):
            dla[k] = part[:, k * 128 : (k + 1) * 128]

    pl.run_scoped(phase2, *acc(C * S, 1), *acc(256, 2))
    for s in range(S):
        for k in range(2):
            dls[s, :, k * 128 : (k + 1) * 128] = dla[k, pl.ds(s, C, stride=S), :].astype(BF)

    def reduce_left(d):
        return to_col(dls.at[col_peer(d)], dlr.at[d - 1], rsl_s, rsl_r, d)

    loop(1, NC, lambda d: reduce_left(d).start())

    def phase3(*accs):
        r_acc = accs[0:4], accs[4:8]
        for q in range(C // 2):
            for m in range(2):
                push(wt[q * 256 : (q + 1) * 256, :], q % 2, m)
                for k in range(4):
                    acc_lhs(r_acc[m][k], tb[4 * m + k, :, q * 256 : (q + 1) * 256], q % 2 if k == 0 else None)
            if q == STAGE_B:
                stage_b()
        for m in range(2):
            for k in range(4):
                at = (4 * m + k) * BLK
                drf[at : at + BLK, :] = pop(r_acc[m][k])[:, :128]

    pl.run_scoped(phase3, *acc(256, 4))

    def reduce_right(d):
        return to_row(drs.at[pl.ds(2 * row_peer(d), 2)], drr.at[d - 1], rsr_s, rsr_r, d)

    def right_piece(d):
        for k in range(2):
            s = 2 * row_peer(d) + k
            drs[s] = drf[pl.ds(s, JL, stride=S), :].T[:C].astype(BF)

    def right_out(d):
        right_piece(d)
        reduce_right(d).start()

    loop(1, NR, right_out)
    right_piece(0)

    loop(1, NC, lambda d: reduce_left(d).wait())
    total = dls[me_c].astype(F32)
    for k in range(NC - 1):
        total += dlr[k].astype(F32)
    dl_out[0] = total * (1.0 / S)
    loop(1, NC, lambda d: weight3(d).wait())
    dw_out[...] = dwg[...]
    loop(1, NR, lambda d: reduce_right(d).wait())
    total = drs[pl.ds(2 * me_r, 2)].astype(F32)
    for k in range(NR - 1):
        total += drr[k].astype(F32)
    dr_out[...] = total * (1.0 / S)


def hand_out(a, b, c, x, y, z):
    x[...] = a[...]
    y[...] = b[...]
    z[...] = c[...].astype(F32)


def on_device(left, right, pair_grad, w_out):
    total_rows = pair_grad.shape[0] * lax.axis_size("row")
    total_cols = pair_grad.shape[1] * lax.axis_size("col")
    scale_weight = 1.0 / (float(total_rows) * float(total_cols)) ** 0.5
    sems = [pltpu.SemaphoreType.DMA((n - 1,)) for n in (NC, NR, NR, NC, NR, NC, NC) for _ in range(2)]
    grads = pl.pallas_call(
        functools.partial(kernel, scale_weight),
        out_shape=(
            pltpu.VMEM((1, C, IL), F32),
            pltpu.VMEM((2, C, JL), F32),
            pltpu.VMEM((C * C, H), BF),
        ),
        in_specs=[pl.BlockSpec(memory_space=pl.ANY)] * 4,
        out_specs=[pl.BlockSpec(memory_space=pltpu.VMEM)] * 3,
        scratch_shapes=[
            pltpu.VMEM((C * C, H), BF),
            pltpu.VMEM((S, C, IL), BF),
            pltpu.VMEM((S, C, JL), BF),
            pltpu.VMEM((NB, IL, JB, H), BF),
            pltpu.VMEM((NB, JB, IL, H), BF),
            pltpu.VMEM((2, C * S, 128), F32),
            pltpu.VMEM((C * S, IL), BF),
            pltpu.VMEM((JL * S, 128), F32),
            pltpu.VMEM((JL * S, 256), BF),
            pltpu.VMEM((C, JL * S), BF),
            pltpu.VMEM((256, C * H), BF),
            pltpu.VMEM((C * H, 256), BF),
            pltpu.VMEM((NB, BLK, C * H), BF),
            pltpu.VMEM((NU, C * S, JB * H), BF),
            pltpu.VMEM((JL * S, 128), F32),
            pltpu.VMEM((S, C, JL), BF),
            pltpu.VMEM((NR - 1, 2, C, JL), BF),
            pltpu.VMEM((C * C, H), BF),
            pltpu.VMEM((NC - 1, 64, H), BF),
            pltpu.VMEM((NR, 64, H), BF),
            pltpu.VMEM((C * C, H), BF),
            pltpu.VMEM((2, C * S, 128), F32),
            pltpu.VMEM((S, C, IL), BF),
            pltpu.VMEM((NC - 1, C, IL), BF),
            pltpu.SemaphoreType.DMA((NB,)),
            pltpu.SemaphoreType.DMA((3,)),
            *sems,
        ],
        compiler_params=pltpu.CompilerParams(
            collective_id=0, has_side_effects=True, vmem_limit_bytes=60 * 2**20
        ),
        name="outer_product_mean_grad",
    )(left, right, pair_grad, w_out)
    return pl.pallas_call(
        hand_out,
        out_shape=tuple(jax.ShapeDtypeStruct(g.shape, F32) for g in grads),
        in_specs=[pl.BlockSpec(memory_space=pltpu.VMEM)] * 3,
        out_specs=[pl.BlockSpec(memory_space=pltpu.VMEM)] * 3,
        name="hand_out",
    )(*[pltpu.with_memory_space_constraint(g, pltpu.VMEM) for g in grads])


def solution(mesh):
    return jax.shard_map(
        on_device,
        mesh=mesh,
        in_specs=(P("col", None, "row"), P("row", None, "col"), P("row", "col", None), P()),
        out_specs=(P("col", None, "row"), P("row", None, "col"), P()),
        check_vma=False,
    )
```

```python
import functools

import jax
import jax.numpy as jnp
from jax import lax
from jax.experimental import pallas as pl
from jax.experimental.pallas import tpu as pltpu
from jax.sharding import PartitionSpec as P

BF, F32 = jnp.bfloat16, jnp.float32
MESH = pl.DeviceIdType.MESH
S, C, H = 16, 32, 128
IL, JL = 256, 128
NR, NC = 8, 16
JB = 16
NB = JL // JB
BLK = JB * S
NU = 5
STAGE_A, STAGE_B = 6, 11
ROWS, COLS = tuple(range(1, NR)), tuple(range(1, NC))


push, acc_lhs, pop = pltpu.matmul_push_rhs, pltpu.matmul_acc_lhs, pltpu.matmul_pop


def acc(rows, count):
    return [pltpu.ACC(m)((rows, 256), F32) for m in range(2) for _ in range(count)]


def each(order, body):
    for k in order:
        body(k)


def loop(lower, upper, body):
    def step(k, carry):
        body(k)
        return carry

    lax.fori_loop(lower, upper, step, 0)


def kernel(
    scale_weight,
    left_hbm, right_hbm, g_hbm, w_hbm,
    dl_out, dr_out, dw_out,
    w_v, lg, rg, g_in, gt, lf, lb, rf, rb, rt, w1, wt, tb, ub,
    drf, drs, drr, dws, dwr1, dwr2, dwg, dla, dls, dlr,
    g_sem, in_sem,
    agl_s, agl_r, agr_s, agr_r, rsr_s, rsr_r, w1_s, w1_r, w2_s, w2_r, w3_s, w3_r, rsl_s, rsl_r,
):
    me_r = lax.axis_index("row")
    me_c = lax.axis_index("col")

    def row_peer(d):
        return lax.rem(me_r + d, NR)

    def col_peer(d):
        return lax.rem(me_c + d, NC)

    def to_row(src, dst, send, recv, d):
        return pltpu.make_async_remote_copy(
            src_ref=src, dst_ref=dst, send_sem=send.at[d - 1], recv_sem=recv.at[d - 1],
            device_id=(row_peer(d), me_c), device_id_type=MESH,
        )

    def to_col(src, dst, send, recv, d):
        return pltpu.make_async_remote_copy(
            src_ref=src, dst_ref=dst, send_sem=send.at[d - 1], recv_sem=recv.at[d - 1],
            device_id=(me_r, col_peer(d)), device_id_type=MESH,
        )

    barrier = pltpu.get_barrier_semaphore()
    each(ROWS, lambda d: pl.semaphore_signal(barrier, inc=1, device_id=(row_peer(d), me_c), device_id_type=MESH))
    each(COLS, lambda d: pl.semaphore_signal(barrier, inc=1, device_id=(me_r, col_peer(d)), device_id_type=MESH))

    def g_copy(b):
        at = pl.multiple_of(b * JB, JB)
        return pltpu.make_async_copy(g_hbm.at[:, pl.ds(at, JB), :], g_in.at[b], g_sem.at[b])

    local = [
        pltpu.make_async_copy(w_hbm, w_v, in_sem.at[0]),
        pltpu.make_async_copy(left_hbm.at[0], lg.at[me_c], in_sem.at[1]),
        pltpu.make_async_copy(right_hbm, rg.at[pl.ds(2 * me_r, 2)], in_sem.at[2]),
    ]
    for copy in local:
        copy.start()
    loop(0, NB, lambda b: g_copy(b).start())
    pl.semaphore_wait(barrier, NR - 1 + NC - 1)

    def gather_left(d):
        return to_col(left_hbm.at[0], lg.at[me_c], agl_s, agl_r, d)

    def gather_right(d):
        return to_row(right_hbm, rg.at[pl.ds(2 * me_r, 2)], agr_s, agr_r, d)

    each(ROWS, lambda d: gather_right(d).start())
    each(COLS, lambda d: gather_left(d).start())

    w1[...] = jnp.zeros_like(w1)
    wt[...] = jnp.zeros_like(wt)
    rb[:, 128:] = jnp.zeros_like(rb[:, 128:])
    local[0].wait()
    for c in range(C):
        w1[:C, c * H : (c + 1) * H] = w_v[c * C : (c + 1) * C, :]
        block = w_v[c * C : (c + 1) * C, :].astype(F32)
        wt[c * H : (c + 1) * H, :128] = jnp.concatenate([block, jnp.zeros((128 - C, H), F32)], 0).T.astype(BF)

    def turn(b):
        g_copy(b).wait()
        for q in range(IL // 16):
            gt[b, :, q * 16 : (q + 1) * 16, :] = jnp.swapaxes(g_in[b, q * 16 : (q + 1) * 16], 0, 1)

    loop(0, NB, turn)

    local[2].wait()
    each(ROWS, lambda d: gather_right(d).wait())
    for s in range(S):
        block = jnp.concatenate([rg[s].astype(F32), jnp.zeros((128 - C, JL), F32)], 0)
        rf[pl.ds(s, JL, stride=S), :] = block.T
    rb[:, :128] = rf[...].astype(BF)

    def right_turned(b):
        at = pl.multiple_of(b * BLK, BLK)
        rt[:, pl.ds(at, BLK)] = rf[pl.ds(at, BLK), :].T[:C].astype(BF)

    loop(0, NB, right_turned)

    def make_u(b, regions):
        at = pl.multiple_of(b * BLK, BLK)
        slot = lax.rem(b, NU)
        pending = []

        def take():
            q = pending.pop(0)
            u = pop(regions[q % 2][q // 2 % 2]).astype(BF)
            for c in range(2):
                for j in range(JB):
                    row = (2 * q + c) * S
                    ub[slot, row : row + S, j * H : (j + 1) * H] = u[j * S : (j + 1) * S, c * H : (c + 1) * H]

        for q in range(C // 2):
            push(w1[:, q * 256 : (q + 1) * 256], q // 2 % 2, q % 2)
            if len(pending) >= 2:
                take()
            acc_lhs(regions[q % 2][q // 2 % 2], rb[pl.ds(at, BLK), :], q // 2 % 2)
            pending.append(q)
        while pending:
            take()

    def early(*accs):
        loop(0, NU, lambda b: make_u(b, (accs[0:2], accs[2:4])))

    pl.run_scoped(early, *acc(256, 2))

    local[1].wait()

    def left_rows(s):
        for k in range(2):
            lf[k, pl.ds(s, C, stride=S), :] = lg[s, :, k * 128 : (k + 1) * 128].astype(F32)

    def left_arrived(d):
        gather_left(d).wait()
        left_rows(lax.rem(me_c + NC - d, NC))

    left_rows(me_c)
    each(COLS, left_arrived)
    for k in range(2):
        lb[:, k * 128 : (k + 1) * 128] = lf[k].astype(BF)

    def pair(b, p):
        return jnp.concatenate([gt[b, 2 * p], gt[b, 2 * p + 1]], 1)

    def phase1(*accs):
        t_acc, w_acc = (accs[0:3], accs[3:6]), (accs[6:14], accs[14:22])

        def block(b):
            at = pl.multiple_of(b * BLK, BLK)
            pending, used = [], [0, 0]

            def take():
                region, p, half = pending.pop(0)
                t = pop(region).astype(BF)
                for k in range(2):
                    j = 2 * p + k
                    for c in range(C // 2):
                        cc = half * (C // 2) + c
                        tb[b, j * S : (j + 1) * S, cc * H : (cc + 1) * H] = t[c * S : (c + 1) * S, k * H : (k + 1) * H]

            for p in range(JB // 2):
                m = p % 2
                push(pair(b, p), p // 2 % 2, m)
                for half in range(2):
                    region = t_acc[m][used[m] % 3]
                    used[m] += 1
                    if len(pending) >= 4:
                        take()
                    acc_lhs(region, lb[half * 256 : (half + 1) * 256, :], p // 2 % 2 if half == 0 else None)
                    pending.append((region, p, half))
            while pending:
                take()
            for q in range(C // 2):
                push(tb[b, :, q * 256 : (q + 1) * 256], q // 2 % 2, q % 2)
                acc_lhs(w_acc[q % 2][q // 2], rt[:, pl.ds(at, BLK)], q // 2 % 2)

        loop(0, NB, block)
        for q in range(C // 2):
            part = pop(w_acc[q % 2][q // 2]).astype(BF)
            for k in range(2):
                dws[(2 * q + k) * C : (2 * q + k + 1) * C, :] = part[:, k * H : (k + 1) * H]

    pl.run_scoped(phase1, *acc(256, 3), *acc(C, 8))

    def weight_rows(k):
        return pl.ds(pl.multiple_of(k * 64, 64), 64)

    def weight1(d):
        return to_col(dws.at[weight_rows(col_peer(d))], dwr1.at[d - 1], w1_s, w1_r, d)

    def weight2(d):
        return to_row(dwr2.at[me_r], dwr2.at[me_r], w2_s, w2_r, d)

    def weight3(d):
        return to_col(dwg.at[weight_rows(me_c)], dwg.at[weight_rows(me_c)], w3_s, w3_r, d)

    each(COLS, lambda d: weight1(d).start())

    def stage_a():
        each(COLS, lambda d: weight1(d).wait())
        total = dws[weight_rows(me_c), :].astype(F32)
        for k in range(NC - 1):
            total += dwr1[k].astype(F32)
        dwr2[me_r] = (total * scale_weight).astype(BF)
        each(ROWS, lambda d: weight2(d).start())

    def stage_b():
        each(ROWS, lambda d: weight2(d).wait())
        total = dwr2[0].astype(F32)
        for k in range(1, NR):
            total += dwr2[k].astype(F32)
        dwg[weight_rows(me_c), :] = total.astype(BF)
        each(COLS, lambda d: weight3(d).start())

    def phase2(*accs):
        l_acc, u_acc = accs[0:2], (accs[2:4], accs[4:6])

        def block(b):
            pl.when(b >= NU)(lambda: make_u(b, u_acc))
            slot = lax.rem(b, NU)
            for p in range(JB // 2):
                push(pair(b, p), p // 2 % 2, p % 2, transpose=True)
                acc_lhs(l_acc[p % 2], ub[slot, :, p * 256 : (p + 1) * 256], p // 2 % 2)
            pl.when(b == STAGE_A)(stage_a)

        loop(0, NB, block)
        part = pop(l_acc[0]) + pop(l_acc[1])
        for k in range(2):
            dla[k] = part[:, k * 128 : (k + 1) * 128]

    pl.run_scoped(phase2, *acc(C * S, 1), *acc(256, 2))
    for s in range(S):
        for k in range(2):
            dls[s, :, k * 128 : (k + 1) * 128] = dla[k, pl.ds(s, C, stride=S), :].astype(BF)

    def reduce_left(d):
        return to_col(dls.at[col_peer(d)], dlr.at[d - 1], rsl_s, rsl_r, d)

    each(COLS, lambda d: reduce_left(d).start())

    def phase3(*accs):
        r_acc = accs[0:4], accs[4:8]
        for q in range(C // 2):
            for m in range(2):
                push(wt[q * 256 : (q + 1) * 256, :], q % 2, m)
                for k in range(4):
                    acc_lhs(r_acc[m][k], tb[4 * m + k, :, q * 256 : (q + 1) * 256], q % 2 if k == 0 else None)
            if q == STAGE_B:
                stage_b()
        for m in range(2):
            for k in range(4):
                at = (4 * m + k) * BLK
                drf[at : at + BLK, :] = pop(r_acc[m][k])[:, :128]

    pl.run_scoped(phase3, *acc(256, 4))

    def reduce_right(d):
        return to_row(drs.at[pl.ds(2 * row_peer(d), 2)], drr.at[d - 1], rsr_s, rsr_r, d)

    def right_piece(d):
        for k in range(2):
            s = 2 * row_peer(d) + k
            drs[s] = drf[pl.ds(s, JL, stride=S), :].T[:C].astype(BF)

    def right_out(d):
        right_piece(d)
        reduce_right(d).start()

    each(ROWS, right_out)
    right_piece(0)

    each(COLS, lambda d: reduce_left(d).wait())
    total = dls[me_c].astype(F32)
    for k in range(NC - 1):
        total += dlr[k].astype(F32)
    dl_out[0] = total * (1.0 / S)
    each(COLS, lambda d: weight3(d).wait())
    dw_out[...] = dwg[...]
    each(ROWS, lambda d: reduce_right(d).wait())
    total = drs[pl.ds(2 * me_r, 2)].astype(F32)
    for k in range(NR - 1):
        total += drr[k].astype(F32)
    dr_out[...] = total * (1.0 / S)


def hand_out(a, b, c, x, y, z):
    x[...] = a[...]
    y[...] = b[...]
    z[...] = c[...].astype(F32)


def on_device(left, right, pair_grad, w_out):
    total_rows = pair_grad.shape[0] * lax.axis_size("row")
    total_cols = pair_grad.shape[1] * lax.axis_size("col")
    scale_weight = 1.0 / (float(total_rows) * float(total_cols)) ** 0.5
    sems = [pltpu.SemaphoreType.DMA((n - 1,)) for n in (NC, NR, NR, NC, NR, NC, NC) for _ in range(2)]
    grads = pl.pallas_call(
        functools.partial(kernel, scale_weight),
        out_shape=(
            pltpu.VMEM((1, C, IL), F32),
            pltpu.VMEM((2, C, JL), F32),
            pltpu.VMEM((C * C, H), BF),
        ),
        in_specs=[pl.BlockSpec(memory_space=pl.ANY)] * 4,
        out_specs=[pl.BlockSpec(memory_space=pltpu.VMEM)] * 3,
        scratch_shapes=[
            pltpu.VMEM((C * C, H), BF),
            pltpu.VMEM((S, C, IL), BF),
            pltpu.VMEM((S, C, JL), BF),
            pltpu.VMEM((NB, IL, JB, H), BF),
            pltpu.VMEM((NB, JB, IL, H), BF),
            pltpu.VMEM((2, C * S, 128), F32),
            pltpu.VMEM((C * S, IL), BF),
            pltpu.VMEM((JL * S, 128), F32),
            pltpu.VMEM((JL * S, 256), BF),
            pltpu.VMEM((C, JL * S), BF),
            pltpu.VMEM((256, C * H), BF),
            pltpu.VMEM((C * H, 256), BF),
            pltpu.VMEM((NB, BLK, C * H), BF),
            pltpu.VMEM((NU, C * S, JB * H), BF),
            pltpu.VMEM((JL * S, 128), F32),
            pltpu.VMEM((S, C, JL), BF),
            pltpu.VMEM((NR - 1, 2, C, JL), BF),
            pltpu.VMEM((C * C, H), BF),
            pltpu.VMEM((NC - 1, 64, H), BF),
            pltpu.VMEM((NR, 64, H), BF),
            pltpu.VMEM((C * C, H), BF),
            pltpu.VMEM((2, C * S, 128), F32),
            pltpu.VMEM((S, C, IL), BF),
            pltpu.VMEM((NC - 1, C, IL), BF),
            pltpu.SemaphoreType.DMA((NB,)),
            pltpu.SemaphoreType.DMA((3,)),
            *sems,
        ],
        compiler_params=pltpu.CompilerParams(
            collective_id=0, has_side_effects=True, vmem_limit_bytes=60 * 2**20
        ),
        name="outer_product_mean_grad",
    )(left, right, pair_grad, w_out)
    return pl.pallas_call(
        hand_out,
        out_shape=tuple(jax.ShapeDtypeStruct(g.shape, F32) for g in grads),
        in_specs=[pl.BlockSpec(memory_space=pltpu.VMEM)] * 3,
        out_specs=[pl.BlockSpec(memory_space=pltpu.VMEM)] * 3,
        name="hand_out",
    )(*[pltpu.with_memory_space_constraint(g, pltpu.VMEM) for g in grads])


def solution(mesh):
    return jax.shard_map(
        on_device,
        mesh=mesh,
        in_specs=(P("col", None, "row"), P("row", None, "col"), P("row", "col", None), P()),
        out_specs=(P("col", None, "row"), P("row", None, "col"), P()),
        check_vma=False,
    )
```
